32 devices in a mesh: row: 4 (over z), col: 4 (over y, x), ka: 2 (over core).
Axes of the slice: x: 2, y: 2, z: 4, core: 2. Of those that a mesh axis runs over, the one named last changes fastest.
Arguments:
- iterate: float32 [2560, 13824], P('row', ('col', 'ka')), may hold values from -0.03125 to 0.03125
Outputs:
- update: bfloat16 [2560, 13824], P('row', ('col', 'ka'))
The draws below stay inside these ranges and needn't reach their ends.
All inputs are finite; a program needn't handle non-finite values.
Results may differ from the reference program's by a relative error of at most 0.02.
Values may be sent and summed in bfloat16 or wider, within the bound.
A program may use at most 64 MiB of HBM per device.

```python
import math
import jax
import jax.numpy as jnp

M = 2560
K = 13824
ITERS = 2


def levels(key, shape, shards, smallest, high):
    factor_of = 1.0
    for dim, blocks in shards:
        steps = jax.random.uniform(jax.random.fold_in(jax.random.fold_in(key, 6), dim), (blocks,), jnp.float32, smallest / len(shards), high / len(shards))
        factor_of = factor_of * jnp.repeat(jnp.exp(steps), shape[dim] // blocks).reshape((-1,) + (1,) * (len(shape) - 1 - dim))
    return factor_of


def bell_draw(stream_key, shape, scale, reach, shards=(), kind=jnp.bfloat16):
    gain = levels(stream_key, shape, shards, -0.22, 0.18) if shards else 1.0
    array = jax.random.normal(stream_key, shape, jnp.float32) * scale * gain
    return jnp.minimum(jnp.maximum(array, -reach), reach).astype(kind)


def setup_inputs(seed: int = 0) -> dict:
    splits = jax.random.split(jax.random.key(seed), 2)
    return {
        "iterate": bell_draw(splits[0], (M, K), (3 * K) ** -0.5, 0.03125, ((0, 4), (1, 8)), jnp.float32),
    }


LINEAR_COEF = 3.4445
CUBIC_COEF = -4.775
QUINTIC_COEF = 2.0315

def reference(iterate):
    current = iterate
    result = None
    for step in range(ITERS):
        rounded = current.astype(jnp.bfloat16)
        gram = jnp.dot(rounded, rounded.T, preferred_element_type=jnp.float32).astype(jnp.bfloat16)
        first = jnp.dot(gram, rounded, preferred_element_type=jnp.float32).astype(jnp.bfloat16)
        second = jnp.dot(gram, first, preferred_element_type=jnp.float32)
        current = LINEAR_COEF * current + CUBIC_COEF * first.astype(jnp.float32) + QUINTIC_COEF * second
    result = (math.sqrt(K) * current).astype(jnp.bfloat16)
    return result
```

```python
import functools
import math

import jax
import jax.numpy as jnp
from jax import lax
from jax.experimental import pallas as pl
from jax.experimental.pallas import tpu as pltpu
from jax.sharding import PartitionSpec as P

LINEAR_COEF = 3.4445
CUBIC_COEF = -4.775
QUINTIC_COEF = 2.0315

MESH = pl.DeviceIdType.MESH


def tile_of(size, most):
    return max(t for t in range(16, min(size, most) + 1, 16) if size % t == 0)


def shifted(value, diagonal, rows, columns):
    r = lax.broadcasted_iota(jnp.int32, value.shape, 0) + rows
    c = lax.broadcasted_iota(jnp.int32, value.shape, 1) + columns
    return value + jnp.where(r == c, jnp.float32(diagonal), jnp.float32(0.0))


def polynomial_kernel(
    mine, u_ref, q_ref, g_ref, p_ref, g1_ref, b_ref, p1_ref, u_sem, p_send, p_recv, g_send, g_recv, q_sems
):
    n = g_ref.shape[0]
    half = n // 2
    columns = tile_of(n, 256)
    steps = n // columns
    ka = lax.axis_index("ka")
    other = {"ka": 1 - ka}
    base = pl.multiple_of(ka * half, 16)
    own = pl.ds(base, half)

    load = pltpu.make_async_copy(u_ref, g1_ref, u_sem)
    load.start()
    barrier = pltpu.get_barrier_semaphore()
    pl.semaphore_signal(barrier, inc=1, device_id=other, device_id_type=MESH)
    pl.semaphore_wait(barrier, 1)

    def exchange(ref, send, recv, step):
        at = ref.at[own, pl.ds(pl.multiple_of(step * columns, columns), columns)]
        return pltpu.make_async_remote_copy(
            src_ref=at,
            dst_ref=at,
            send_sem=send.at[step],
            recv_sem=recv.at[step],
            device_id=other,
            device_id_type=MESH,
        )

    def loop_columns(body):
        @pl.loop(0, steps)
        def _(j):
            body(j, pl.ds(pl.multiple_of(j * columns, columns), columns), j * columns)

    load.wait()

    @pl.loop(0, steps)
    def _(i):
        above = pl.ds(pl.multiple_of(i * columns, columns), columns)

        @pl.loop(i, steps)
        def _(j):
            left = pl.ds(pl.multiple_of(j * columns, columns), columns)
            value = g1_ref[above, left].astype(jnp.float32) + g1_ref[left, above].astype(jnp.float32).T
            g_ref[above, left] = value.astype(jnp.bfloat16)
            g_ref[left, above] = value.T.astype(jnp.bfloat16)

    def tile_p0(j, cols, start):
        square = jnp.dot(g_ref[own, :], g_ref[:, cols], preferred_element_type=jnp.float32)
        value = CUBIC_COEF * g_ref[own, cols].astype(jnp.float32) + QUINTIC_COEF * square
        p_ref[own, cols] = shifted(value, LINEAR_COEF, base, start).astype(jnp.bfloat16)
        exchange(p_ref, p_send, p_recv, j).start()

    loop_columns(tile_p0)
    for j in range(steps):
        exchange(p_ref, p_send, p_recv, j).wait()

    def tile_b(j, cols, start):
        value = jnp.dot(g_ref[own, :], p_ref[:, cols], preferred_element_type=jnp.float32)
        b_ref[:, cols] = value.astype(jnp.bfloat16)

    loop_columns(tile_b)

    def tile_g1(j, cols, start):
        value = jnp.dot(b_ref[...], p_ref[:, cols], preferred_element_type=jnp.float32)
        g1_ref[own, cols] = value.astype(jnp.bfloat16)
        exchange(g1_ref, g_send, g_recv, j).start()

    loop_columns(tile_g1)
    for j in range(steps):
        exchange(g1_ref, g_send, g_recv, j).wait()

    part = mine // 2
    first = pl.multiple_of(lax.axis_index("row") * mine + ka * part, 16)

    def tile_p1(j, cols, start):
        square = jnp.dot(g1_ref[pl.ds(first, part), :], g1_ref[:, cols], preferred_element_type=jnp.float32)
        value = CUBIC_COEF * g1_ref[pl.ds(first, part), cols].astype(jnp.float32) + QUINTIC_COEF * square
        p1_ref[:, cols] = shifted(value, LINEAR_COEF, first, start).astype(jnp.bfloat16)

    loop_columns(tile_p1)

    here = pl.ds(pl.multiple_of(ka * part, 16), part)

    def tile_q(j, cols, start):
        value = jnp.dot(p1_ref[...], p_ref[:, cols], preferred_element_type=jnp.float32)
        q_ref[here, cols] = value.astype(jnp.bfloat16)

    loop_columns(tile_q)
    copy = pltpu.make_async_remote_copy(
        src_ref=q_ref.at[here, :],
        dst_ref=q_ref.at[here, :],
        send_sem=q_sems.at[0],
        recv_sem=q_sems.at[1],
        device_id=other,
        device_id_type=MESH,
    )
    copy.start()
    copy.wait()


def polynomial(share, mine):
    n = share.shape[0]
    half = n // 2
    steps = n // tile_of(n, 256)
    dma = pltpu.SemaphoreType.DMA
    return pl.pallas_call(
        functools.partial(polynomial_kernel, mine),
        out_shape=jax.ShapeDtypeStruct((mine, n), jnp.bfloat16),
        in_specs=[pl.BlockSpec(memory_space=pl.ANY)],
        out_specs=pl.BlockSpec(memory_space=pltpu.VMEM),
        scratch_shapes=[
            pltpu.VMEM((n, n), jnp.bfloat16),
            pltpu.VMEM((n, n), jnp.bfloat16),
            pltpu.VMEM((n, n), jnp.bfloat16),
            pltpu.VMEM((half, n), jnp.bfloat16),
            pltpu.VMEM((mine // 2, n), jnp.bfloat16),
            dma,
            dma((steps,)),
            dma((steps,)),
            dma((steps,)),
            dma((steps,)),
            dma((2,)),
        ],
        compiler_params=pltpu.CompilerParams(
            collective_id=0, has_side_effects=True, vmem_limit_bytes=60 * 1024 * 1024
        ),
        cost_estimate=pl.CostEstimate(
            flops=2 * n * n * (3 * half + mine), bytes_accessed=2 * n * (n + mine), transcendentals=0
        ),
        name="polynomial",
    )(share)


def rows_dot(left, right):
    return lax.dot_general(left, right, (((1,), (1,)), ((), ())), preferred_element_type=jnp.float32)


def body(scale, count, iterate):
    mine, width = iterate.shape
    n = mine * count
    middle = count // 2
    z = lax.axis_index("row")
    upper = z >= middle

    def from_ahead(value, distance):
        return lax.ppermute(value, "row", [((i + distance) % count, i) for i in range(count)])

    rounded = iterate.astype(jnp.bfloat16)
    low, high = rounded[:, : width // 2], rounded[:, width // 2 :]
    ahead = [from_ahead(rounded, d) for d in range(1, middle)]
    far = from_ahead(jnp.where(upper, low, high), middle)
    strip = [0.5 * rows_dot(rounded, rounded)]
    strip += [rows_dot(rounded, block) for block in ahead]
    strip.append(rows_dot(jnp.where(upper, high, low), far))
    partial = jnp.concatenate([part.astype(jnp.bfloat16) for part in strip], axis=1)

    later, _ = lax.optimization_barrier((rounded, (ahead, far)))
    later_low, later_high = later[:, : width // 2], later[:, width // 2 :]
    far_rest = from_ahead(jnp.where(upper, later_high, later_low), middle)
    behind = [from_ahead(later, d) for d in range(middle + 1, count)]

    block = lax.psum_scatter(partial, ("col", "ka"), scatter_dimension=0, tiled=True)
    strips = lax.all_gather(block, ("row", "col", "ka"), axis=0, tiled=True)
    shares = []
    for i in range(count):
        share = jnp.pad(strips[i * mine : (i + 1) * mine], ((0, 0), (0, n - strips.shape[1])))
        shares.append(jnp.roll(share, i * mine, axis=1))
    share = jnp.concatenate(shares, axis=0)
    q = polynomial(share, mine)
    from_here = lax.dynamic_slice_in_dim(jnp.concatenate([q, q], axis=1), z * mine, n, axis=1)
    far_low, far_high = jnp.where(upper, far_rest, far), jnp.where(upper, far, far_rest)
    opposite = jnp.concatenate([far_low, far_high], axis=1)
    gathered = jnp.concatenate([rounded, *ahead, opposite, *behind], axis=0)
    update = jnp.dot(from_here, gathered, preferred_element_type=jnp.float32)
    return (scale * update).astype(jnp.bfloat16)


def solution(mesh):
    spec = P("row", ("col", "ka"))

    def whole(iterate):
        scale = math.sqrt(iterate.shape[1])
        return jax.shard_map(
            functools.partial(body, scale, mesh.shape["row"]), mesh=mesh, in_specs=(spec,), out_specs=spec, check_vma=False
        )(iterate)

    return whole
```

```python
import functools
import math

import jax
import jax.numpy as jnp
from jax import lax
from jax.experimental import pallas as pl
from jax.experimental.pallas import tpu as pltpu
from jax.sharding import PartitionSpec as P

LINEAR_COEF = 3.4445
CUBIC_COEF = -4.775
QUINTIC_COEF = 2.0315

MESH = pl.DeviceIdType.MESH


def tile_of(size, most):
    return max(t for t in range(16, min(size, most) + 1, 16) if size % t == 0)


def shifted(value, diagonal, rows, columns):
    r = lax.broadcasted_iota(jnp.int32, value.shape, 0) + rows
    c = lax.broadcasted_iota(jnp.int32, value.shape, 1) + columns
    return value + jnp.where(r == c, jnp.float32(diagonal), jnp.float32(0.0))


def polynomial_kernel(
    mine, packed, u_ref, x_ref, q_ref, behind_ref, g_ref, p_ref, g1_ref, b_ref, p1_ref, u_sem, x_send, x_recv,
    p_send, p_recv, g_send, g_recv, q_sems
):
    n = g_ref.shape[0]
    half = n // 2
    columns = tile_of(n, 256)
    steps = n // columns
    ka = lax.axis_index("ka")
    other = {"ka": 1 - ka}
    base = pl.multiple_of(ka * half, 16)
    own = pl.ds(base, half)

    loads = []
    if packed:
        count = n // mine
        kept = u_ref.shape[1] // mine
        for i in range(count):
            for d in range(count):
                j = (i + d) % count
                at = g1_ref.at[i * mine : (i + 1) * mine, j * mine : (j + 1) * mine]
                if d < kept:
                    block = u_ref.at[i * mine : (i + 1) * mine, d * mine : (d + 1) * mine]
                    loads.append(pltpu.make_async_copy(block, at, u_sem.at[i * kept + d]))
                    loads[-1].start()
                else:
                    at[...] = jnp.zeros((mine, mine), jnp.bfloat16)
    else:
        loads.append(pltpu.make_async_copy(u_ref, g1_ref, u_sem.at[0]))
        loads[-1].start()
    barrier = pltpu.get_barrier_semaphore()
    pl.semaphore_signal(barrier, inc=1, device_id=other, device_id_type=MESH)
    z, count, slots = lax.axis_index("row"), n // mine, behind_ref.shape[0]
    targets = [{"row": lax.rem(z + s + 1, count)} for s in range(slots)]
    sources = [{"row": lax.rem(z + count - s - 1, count)} for s in range(slots)]
    for device in targets + sources:
        pl.semaphore_signal(barrier, inc=1, device_id=device, device_id_type=MESH)
    pl.semaphore_wait(barrier, 1 + 2 * slots)

    sends = [
        pltpu.make_async_remote_copy(
            src_ref=x_ref,
            dst_ref=behind_ref.at[s],
            send_sem=x_send.at[s],
            recv_sem=x_recv.at[s],
            device_id=targets[s],
            device_id_type=MESH,
        )
        for s in range(slots)
    ]
    for send in sends:
        send.start()

    def exchange(ref, send, recv, step):
        at = ref.at[own, pl.ds(pl.multiple_of(step * columns, columns), columns)]
        return pltpu.make_async_remote_copy(
            src_ref=at,
            dst_ref=at,
            send_sem=send.at[step],
            recv_sem=recv.at[step],
            device_id=other,
            device_id_type=MESH,
        )

    def loop_columns(body):
        @pl.loop(0, steps)
        def _(j):
            body(j, pl.ds(pl.multiple_of(j * columns, columns), columns), j * columns)

    for load in loads:
        load.wait()

    @pl.loop(0, steps)
    def _(i):
        above = pl.ds(pl.multiple_of(i * columns, columns), columns)

        @pl.loop(i, steps)
        def _(j):
            left = pl.ds(pl.multiple_of(j * columns, columns), columns)
            value = g1_ref[above, left].astype(jnp.float32) + g1_ref[left, above].astype(jnp.float32).T
            g_ref[above, left] = value.astype(jnp.bfloat16)
            g_ref[left, above] = value.T.astype(jnp.bfloat16)

    def tile_p0(j, cols, start):
        square = jnp.dot(g_ref[own, :], g_ref[:, cols], preferred_element_type=jnp.float32)
        value = CUBIC_COEF * g_ref[own, cols].astype(jnp.float32) + QUINTIC_COEF * square
        p_ref[own, cols] = shifted(value, LINEAR_COEF, base, start).astype(jnp.bfloat16)
        exchange(p_ref, p_send, p_recv, j).start()

    loop_columns(tile_p0)
    for j in range(steps):
        exchange(p_ref, p_send, p_recv, j).wait()

    def tile_b(j, cols, start):
        value = jnp.dot(g_ref[own, :], p_ref[:, cols], preferred_element_type=jnp.float32)
        b_ref[:, cols] = value.astype(jnp.bfloat16)

    loop_columns(tile_b)

    def tile_g1(j, cols, start):
        value = jnp.dot(b_ref[...], p_ref[:, cols], preferred_element_type=jnp.float32)
        g1_ref[own, cols] = value.astype(jnp.bfloat16)
        exchange(g1_ref, g_send, g_recv, j).start()

    loop_columns(tile_g1)
    for j in range(steps):
        exchange(g1_ref, g_send, g_recv, j).wait()

    part = mine // 2
    first = pl.multiple_of(lax.axis_index("row") * mine + ka * part, 16)

    def tile_p1(j, cols, start):
        square = jnp.dot(g1_ref[pl.ds(first, part), :], g1_ref[:, cols], preferred_element_type=jnp.float32)
        value = CUBIC_COEF * g1_ref[pl.ds(first, part), cols].astype(jnp.float32) + QUINTIC_COEF * square
        p1_ref[:, cols] = shifted(value, LINEAR_COEF, first, start).astype(jnp.bfloat16)

    loop_columns(tile_p1)

    here = pl.ds(pl.multiple_of(ka * part, 16), part)

    if packed:

        @pl.loop(0, n // mine)
        def _(d):
            source = lax.rem(lax.axis_index("row") + d, n // mine)
            cols = pl.ds(pl.multiple_of(source * mine, 128), mine)
            value = jnp.dot(p1_ref[...], p_ref[:, cols], preferred_element_type=jnp.float32)
            q_ref[here, pl.ds(pl.multiple_of(d * mine, 128), mine)] = value.astype(jnp.bfloat16)
    else:

        def tile_q(j, cols, start):
            value = jnp.dot(p1_ref[...], p_ref[:, cols], preferred_element_type=jnp.float32)
            q_ref[here, cols] = value.astype(jnp.bfloat16)

        loop_columns(tile_q)
    copy = pltpu.make_async_remote_copy(
        src_ref=q_ref.at[here, :],
        dst_ref=q_ref.at[here, :],
        send_sem=q_sems.at[0],
        recv_sem=q_sems.at[1],
        device_id=other,
        device_id_type=MESH,
    )
    copy.start()
    copy.wait()
    for send in sends:
        send.wait()


def polynomial(share, turned, packed):
    n = share.shape[0]
    width, mine = turned.shape
    slots = n // mine - n // mine // 2 - 1
    half = n // 2
    steps = n // tile_of(n, 256)
    dma = pltpu.SemaphoreType.DMA
    return pl.pallas_call(
        functools.partial(polynomial_kernel, mine, packed),
        out_shape=(
            jax.ShapeDtypeStruct((mine, n), jnp.bfloat16),
            jax.ShapeDtypeStruct((slots, width, mine), jnp.bfloat16),
        ),
        in_specs=[pl.BlockSpec(memory_space=pl.ANY)] * 2,
        out_specs=(pl.BlockSpec(memory_space=pltpu.VMEM), pl.BlockSpec(memory_space=pl.ANY)),
        scratch_shapes=[
            pltpu.VMEM((n, n), jnp.bfloat16),
            pltpu.VMEM((n, n), jnp.bfloat16),
            pltpu.VMEM((n, n), jnp.bfloat16),
            pltpu.VMEM((half, n), jnp.bfloat16),
            pltpu.VMEM((mine // 2, n), jnp.bfloat16),
            dma(((n // mine) * (share.shape[1] // mine) if packed else 1,)),
            dma((slots,)),
            dma((slots,)),
            dma((steps,)),
            dma((steps,)),
            dma((steps,)),
            dma((steps,)),
            dma((2,)),
        ],
        compiler_params=pltpu.CompilerParams(
            collective_id=0, has_side_effects=True, vmem_limit_bytes=60 * 1024 * 1024
        ),
        cost_estimate=pl.CostEstimate(
            flops=2 * n * n * (3 * half + mine), bytes_accessed=2 * n * (n + mine), transcendentals=0
        ),
        name="polynomial",
    )(share, turned)


def rows_dot(left, right):
    return lax.dot_general(left, right, (((1,), (1,)), ((), ())), preferred_element_type=jnp.float32)


def body(scale, count, iterate):
    mine, width = iterate.shape
    n = mine * count
    middle = count // 2
    z = lax.axis_index("row")
    upper = z >= middle

    def from_ahead(value, distance):
        return lax.ppermute(value, "row", [((i + distance) % count, i) for i in range(count)])

    rounded = iterate.astype(jnp.bfloat16)
    low, high = rounded[:, : width // 2], rounded[:, width // 2 :]
    ahead = [from_ahead(rounded, d) for d in range(1, middle)]
    far = from_ahead(jnp.where(upper, low, high), middle)
    strip = [0.5 * rows_dot(rounded, rounded)]
    strip += [rows_dot(rounded, block) for block in ahead]
    strip.append(rows_dot(jnp.where(upper, high, low), far))
    partial = jnp.concatenate([part.astype(jnp.bfloat16) for part in strip], axis=1)

    later, _ = lax.optimization_barrier((rounded, (ahead, far)))
    later_low, later_high = later[:, : width // 2], later[:, width // 2 :]
    far_rest = from_ahead(jnp.where(upper, later_high, later_low), middle)

    block = lax.psum_scatter(partial, ("col", "ka"), scatter_dimension=0, tiled=True)
    block, far_rest = lax.optimization_barrier((block, far_rest))
    strips = lax.all_gather(block, ("row", "col", "ka"), axis=0, tiled=True)
    packed = mine % 128 == 0
    if packed:
        q, behind = polynomial(strips, rounded.T, packed)
    else:
        shares = []
        for i in range(count):
            share = jnp.pad(strips[i * mine : (i + 1) * mine], ((0, 0), (0, n - strips.shape[1])))
            shares.append(jnp.roll(share, i * mine, axis=1))
        q, behind = polynomial(jnp.concatenate(shares, axis=0), rounded.T, packed)
        q = lax.dynamic_slice_in_dim(jnp.concatenate([q, q], axis=1), z * mine, n, axis=1)

    far_low, far_high = jnp.where(upper, far_rest, far), jnp.where(upper, far, far_rest)
    opposite = jnp.concatenate([far_low, far_high], axis=1)
    blocks = [rounded, *ahead, opposite] + [behind[s].T for s in reversed(range(behind.shape[0]))]
    update = 0.0
    for d, rows in enumerate(blocks):
        update += jnp.dot(q[:, d * mine : (d + 1) * mine], rows, preferred_element_type=jnp.float32)
    return (scale * update).astype(jnp.bfloat16)


def solution(mesh):
    spec = P("row", ("col", "ka"))

    def whole(iterate):
        scale = math.sqrt(iterate.shape[1])
        return jax.shard_map(
            functools.partial(body, scale, mesh.shape["row"]), mesh=mesh, in_specs=(spec,), out_specs=spec, check_vma=False
        )(iterate)

    return whole
```
